256 devices in a mesh: dp: 16 (over z_hi, x), ctx: 16 (over y, z_lo, core).
Axes of the slice: x: 4, y: 4, z: 8 (z_hi: 4, z_lo: 2; z = z_hi * 2 + z_lo), core: 2. Of those that a mesh axis runs over, the one named last changes fastest.
Arguments:
- doc_lengths: int32 [64], replicated, may hold values from 1 to 1792, 65536 in all
- queries: bfloat16 [65536, 1024], P(('dp', 'ctx')), may hold values from -6 to 6
- key_rows: bfloat16 [65536, 128], P(('dp', 'ctx')), may hold values from -6 to 6
- value_rows: bfloat16 [65536, 128], P(('dp', 'ctx')), may hold values from -6 to 6
- grad_out: bfloat16 [65536, 1024], P(('dp', 'ctx')), may hold values from -6 to 6
Outputs:
- attn_out: bfloat16 [65536, 1024], P(('dp', 'ctx'))
- grad_queries: bfloat16 [65536, 1024], P(('dp', 'ctx'))
- grad_keys: bfloat16 [65536, 128], P(('dp', 'ctx'))
- grad_values: bfloat16 [65536, 128], P(('dp', 'ctx'))
The draws below stay inside these ranges and needn't reach their ends.
Inputs may be any that keep to these rules, and one draw needn't show every extreme that they name: `doc_lengths`: the lengths sum to 65536; each is at most 1792, and one document has exactly 1792 tokens.
All inputs are finite; a program needn't handle non-finite values.
Results may differ from the reference program's by a relative error of at most 0.034.
Values may be sent and summed in bfloat16 or wider, within the bound.
No kernel may reach another device: no remote copies, remote signals or barrier semaphores. Data moves between devices by JAX's collectives and lax.ppermute only.
A program may use at most 64 MiB of HBM per device.

```python
import math
import jax
import jax.numpy as jnp
import numpy as np
from jax import lax

HEADS = 8
HDIM = 128
T_DEV = 256
REACH = 8
NDOC = 64
MOST = 1792
TOKENS = 65536


def draw_queries(key, part):
    key = jax.random.fold_in(key, 11)
    base = jnp.clip(jax.random.normal(key, (TOKENS, HEADS * HDIM), jnp.float32), -6.0, 6.0)
    return base.astype(jnp.bfloat16)


def draw_key_rows(key, part):
    key = jax.random.fold_in(key, 23)
    base = jnp.clip(jax.random.normal(key, (TOKENS, HDIM), jnp.float32), -6.0, 6.0)
    return base.astype(jnp.bfloat16)


def level_of(stream_key, dims, cuts, low, largest):
    def one(dim, parts):
        steps = jax.random.uniform(jax.random.fold_in(jax.random.fold_in(stream_key, 6), dim), (parts,), jnp.float32, low / len(cuts), largest / len(cuts))
        return jnp.repeat(jnp.exp(steps), dims[dim] // parts).reshape((-1,) + (1,) * (len(dims) - dim - 1))

    loudness = one(*cuts[0])
    for cut in cuts[1:]:
        loudness = loudness * one(*cut)
    return loudness


def profile(count, total, bound, slope):
    weights = [(1 << 20) // math.isqrt(grade ** slope) + 1 for grade in range(2, count + 1)]
    rest, counts = total - bound - (count - 1), [1] * (count - 1)
    while rest > 0:
        movable = [i for i in range(count - 1) if counts[i] < bound]
        whole, budget = sum([weights[i] for i in movable]), rest
        for i in movable:
            addition = min(bound - counts[i], max(1, budget * weights[i] // whole), rest)
            counts[i] = counts[i] + addition
            rest = rest - addition
    return np.array([bound] + counts)


def ragged_sizes(rng, number_of, total, limit, lean):
    if number_of == 2:
        one = jax.random.randint(rng, (), max(1, total - limit), min(limit, total - 1) + 1)
        return jnp.stack([one, total - one])
    sizes = jnp.asarray(profile(number_of, total, limit, lean), jnp.int32)
    couples = (number_of - 1) // 2
    source_of, sink = sizes[1:1 + 2 * couples:2], sizes[2:2 + 2 * couples:2]
    room = jnp.minimum(source_of - 1, limit - sink)
    passed = jax.random.randint(jax.random.fold_in(rng, 1), (couples,), 0, 1 << 20) % (room + 1)
    sizes = sizes.at[1:1 + 2 * couples:2].set(source_of - passed).at[2:2 + 2 * couples:2].set(sink + passed)
    return sizes[jax.random.permutation(jax.random.fold_in(rng, 2), number_of)]


def normal_values(stream_key, shape, width, reach, cuts=(), kind=jnp.bfloat16):
    result = jax.random.normal(stream_key, shape, jnp.float32) * width
    if len(cuts) > 0:
        result = level_of(stream_key, shape, cuts, -0.22, 0.18) * result
    return jnp.clip(result, min=-reach, max=reach).astype(kind)


def setup_inputs(seed: int = 0) -> dict:
    arg_keys = jax.random.split(jax.random.key(seed), 6)
    return {
        "doc_lengths": ragged_sizes(arg_keys[0], NDOC, TOKENS, MOST, 2).astype(jnp.int32),
        "queries": draw_queries(jax.random.fold_in(arg_keys[5], 71), 0),
        "key_rows": draw_key_rows(jax.random.fold_in(arg_keys[5], 71), 0),
        "value_rows": normal_values(arg_keys[3], (TOKENS, HDIM), 1.0, 6.0, ((0, 256),)),
        "grad_out": normal_values(arg_keys[4], (TOKENS, HEADS * HDIM), 1.0, 6.0, ((0, 256),)),
    }


def attend_block(q_block, win_keys, win_values, g_block, q_pos, key_pos, q_begin, head_count, head_size):
    tokens_here = q_block.shape[0]
    span_len = win_keys.shape[0]
    scale = head_size ** -0.5
    query_rows = q_block.reshape(tokens_here * head_count, head_size)
    grad_rows = g_block.reshape(tokens_here * head_count, head_size)
    scores = jnp.dot(query_rows, win_keys.T, preferred_element_type=jnp.float32) * scale
    scores = scores.reshape(tokens_here, head_count, span_len)
    allowed = (key_pos[None, :] <= q_pos[:, None]) & (key_pos[None, :] >= q_begin[:, None])
    scores = jnp.where(allowed[:, None, :], scores, -jnp.inf)
    row_max = jnp.max(scores, axis=2, keepdims=True)
    weights = jnp.exp(scores - row_max)
    row_sum = jnp.sum(weights, axis=2, keepdims=True)
    weights_bf = weights.astype(jnp.bfloat16).reshape(tokens_here * head_count, span_len)
    out_rows = (jnp.dot(weights_bf, win_values, preferred_element_type=jnp.float32) / row_sum.reshape(-1, 1)).astype(jnp.bfloat16)
    row_dot = jnp.sum(grad_rows.astype(jnp.float32) * out_rows.astype(jnp.float32), axis=1)
    probs = (weights / row_sum).reshape(tokens_here * head_count, span_len)
    probs_bf = probs.astype(jnp.bfloat16)
    grad_probs = jnp.dot(grad_rows, win_values.T, preferred_element_type=jnp.float32)
    grad_scores = (probs * (grad_probs - row_dot[:, None])).astype(jnp.bfloat16)
    grad_query = (jnp.dot(grad_scores, win_keys, preferred_element_type=jnp.float32) * scale).astype(jnp.bfloat16)
    grad_key = jnp.dot(grad_scores.T, query_rows, preferred_element_type=jnp.float32) * scale
    grad_value = jnp.dot(probs_bf.T, grad_rows, preferred_element_type=jnp.float32)
    return (out_rows.reshape(tokens_here, head_count * head_size), grad_query.reshape(tokens_here, head_count * head_size), grad_key, grad_value)


def begin_of(doc_starts, positions):
    return jnp.max(jnp.where(doc_starts[None, :] <= positions[:, None], doc_starts[None, :], 0), axis=1).astype(jnp.int32)


def round_remote(terms, margin):
    remote = lax.optimization_barrier(terms[:margin].astype(jnp.bfloat16))
    return jnp.concatenate([remote.astype(jnp.float32), terms[margin:]], axis=0)


def reference(doc_lengths, queries, key_rows, value_rows, grad_out):
    margin = (REACH - 1) * T_DEV
    window = REACH * T_DEV
    doc_starts = (jnp.cumsum(doc_lengths) - doc_lengths).astype(jnp.int32)
    pad_keys = jnp.concatenate([jnp.zeros((margin, HDIM), key_rows.dtype), key_rows])
    pad_values = jnp.concatenate([jnp.zeros((margin, HDIM), value_rows.dtype), value_rows])
    block_total = TOKENS // T_DEV
    q_blocks = queries.reshape(block_total, T_DEV, HEADS * HDIM)
    g_blocks = grad_out.reshape(block_total, T_DEV, HEADS * HDIM)

    def fold_step(totals, item):
        sum_keys, sum_values = totals
        block_id, q_block, g_block = item
        first_row = (block_id * T_DEV).astype(jnp.int32)
        q_pos = first_row + jnp.arange(T_DEV, dtype=jnp.int32)
        key_pos = first_row - margin + jnp.arange(window, dtype=jnp.int32)
        win_keys = lax.dynamic_slice_in_dim(pad_keys, first_row, window, 0)
        win_values = lax.dynamic_slice_in_dim(pad_values, first_row, window, 0)
        q_begin = begin_of(doc_starts, q_pos)
        out_rows, grad_query, grad_key, grad_value = attend_block(q_block, win_keys, win_values, g_block, q_pos, key_pos, q_begin, HEADS, HDIM)
        grad_key = round_remote(grad_key, margin)
        grad_value = round_remote(grad_value, margin)
        sum_keys = lax.dynamic_update_slice_in_dim(sum_keys, lax.dynamic_slice_in_dim(sum_keys, first_row, window, 0) + grad_key, first_row, 0)
        sum_values = lax.dynamic_update_slice_in_dim(sum_values, lax.dynamic_slice_in_dim(sum_values, first_row, window, 0) + grad_value, first_row, 0)
        return (sum_keys, sum_values), (out_rows, grad_query)

    empty = jnp.zeros((TOKENS + margin, HDIM), jnp.float32)
    totals, stacked = lax.scan(fold_step, (empty, empty), (jnp.arange(block_total, dtype=jnp.int32), q_blocks, g_blocks))
    attn_out = stacked[0].reshape(TOKENS, HEADS * HDIM)
    grad_queries = stacked[1].reshape(TOKENS, HEADS * HDIM)
    grad_keys = totals[0][margin:].astype(jnp.bfloat16)
    grad_values = totals[1][margin:].astype(jnp.bfloat16)
    return (attn_out, grad_queries, grad_keys, grad_values)
```

```python
import math

import jax
import jax.numpy as jnp
from jax import lax
from jax.experimental import pallas as pl
from jax.experimental.pallas import tpu as pltpu
from jax.sharding import PartitionSpec as P

REACH = 8
AXES = ("dp", "ctx")
F32 = jnp.float32
BF16 = jnp.bfloat16
BIG = 1e30


def cyclic(value, steps):
    count = lax.axis_size(AXES)
    return lax.ppermute(value, AXES, [(s, (s + steps) % count) for s in range(count)])


def swapped(value, bit):
    count = lax.axis_size(AXES)
    return lax.ppermute(value, AXES, [(s, s ^ bit) for s in range(count)])


def dot(a, b):
    return jnp.dot(a, b, preferred_element_type=F32)


def attend_kernel(
    first_ref, ends_ref, q_ref, g_ref, own_ref, four_ref, two_ref, odd_ref,
    o_ref, dq_ref, even_ref, far_ref,
    kaug, k_t, v_t, f_t, s_ref, w_all, ds_all, q_div, g_div,
):
    tokens, dim = own_ref.shape[1:]
    heads = q_ref.shape[1] // dim
    window = REACH * tokens
    scale = dim ** -0.5
    first = first_ref[0]
    blocks = [
        odd_ref.at[3], two_ref.at[1], odd_ref.at[2], four_ref,
        odd_ref.at[1], two_ref.at[0], odd_ref.at[0], own_ref,
    ]
    ends = ends_ref[0:1, :]
    starts = ends_ref[1:2, :]
    docs = ends_ref.shape[1]
    for b, block in enumerate(blocks):
        rows = slice(b * tokens, (b + 1) * tokens)
        at = first - (REACH - 1 - b) * tokens + lax.broadcasted_iota(jnp.int32, (tokens, docs), 0)
        inside = (at >= starts) & (at < ends)
        kaug[rows, :dim] = block[0]
        kaug[rows, dim:] = jnp.where(inside, 1.0, 0.0).astype(BF16)
        k_t[:, rows] = block[0].T
        v_t[:, rows] = block[1].T
    f_t[...] = jnp.where(inside, 0.0, -BIG).T.astype(BF16)
    causal = lax.broadcasted_iota(jnp.int32, (tokens, tokens), 0) <= lax.broadcasted_iota(
        jnp.int32, (tokens, tokens), 1
    )

    def head(h, carry):
        cols = pl.ds(pl.multiple_of(h * dim, dim), dim)
        span = pl.ds(pl.multiple_of(h * tokens, tokens), tokens)
        q = q_ref[:, cols]
        g = g_ref[:, cols]
        g_t = g.T
        q_aug = jnp.concatenate([q.T, f_t[...]], axis=0)
        top = jnp.full((8, tokens), -jnp.inf, F32)
        for b in range(REACH):
            rows = slice(b * tokens, (b + 1) * tokens)
            s = dot(kaug[rows, :], q_aug)
            if b == REACH - 1:
                s = jnp.where(causal, s, -BIG)
            s_ref[rows, :] = s
            top = jnp.maximum(top, jnp.max(s.reshape(tokens // 8, 8, tokens), axis=0))
        unit = scale * math.log2(math.e)
        row_max = jnp.max(top, axis=0, keepdims=True) * unit
        total = jnp.zeros((8, tokens), F32)
        for b in range(REACH):
            rows = slice(b * tokens, (b + 1) * tokens)
            w = jnp.exp2(s_ref[rows, :] * unit - row_max)
            total = total + jnp.sum(w.reshape(tokens // 8, 8, tokens), axis=0)
            s_ref[rows, :] = w
            w_all[rows, span] = w.astype(BF16)
        inv = 1.0 / jnp.sum(total, axis=0, keepdims=True)
        o_t = dot(v_t[...], w_all[:, span]) * inv
        o_ref[:, cols] = o_t.T.astype(BF16)
        row_dot = jnp.sum(g_t.astype(F32) * o_t.astype(BF16).astype(F32), axis=0, keepdims=True)
        inv_col = jnp.broadcast_to(inv, (dim, tokens)).T
        g_div[span, :] = (g.astype(F32) * inv_col).astype(BF16)
        q_div[span, :] = (q.astype(F32) * inv_col).astype(BF16)
        for b, block in enumerate(blocks):
            rows = slice(b * tokens, (b + 1) * tokens)
            ds = s_ref[rows, :] * (dot(block[1], g_t) - row_dot)
            ds_all[rows, span] = ds.astype(BF16)
        dq_t = dot(k_t[...], ds_all[:, span]) * (inv * scale)
        dq_ref[:, cols] = dq_t.T.astype(BF16)
        return carry

    lax.fori_loop(0, heads, head, 0)
    for b in range(REACH):
        rows = slice(b * tokens, (b + 1) * tokens)
        back = REACH - 1 - b
        out, slot = (far_ref, back // 2) if back % 2 else (even_ref, back // 2)
        out[slot, 0] = (dot(ds_all[rows, :], q_div[...]) * scale).astype(out.dtype)
        out[slot, 1] = dot(w_all[rows, :], g_div[...]).astype(out.dtype)


def attend(first, ends, queries, grad_out, own, four, two, odd):
    tokens, dim = own.shape[1:]
    width = queries.shape[1]
    heads = width // dim
    window = REACH * tokens
    vmem = pl.BlockSpec(memory_space=pltpu.VMEM)
    half = REACH // 2
    return pl.pallas_call(
        attend_kernel,
        out_shape=(
            jax.ShapeDtypeStruct((tokens, width), BF16),
            jax.ShapeDtypeStruct((tokens, width), BF16),
            jax.ShapeDtypeStruct((half, 2, tokens, dim), F32),
            jax.ShapeDtypeStruct((half, 2, tokens, dim), BF16),
        ),
        in_specs=[pl.BlockSpec(memory_space=pltpu.SMEM)] + [vmem] * 7,
        out_specs=(vmem,) * 4,
        scratch_shapes=[
            pltpu.VMEM((window, 2 * dim), BF16),
            pltpu.VMEM((dim, window), BF16),
            pltpu.VMEM((dim, window), BF16),
            pltpu.VMEM((dim, tokens), BF16),
            pltpu.VMEM((window, tokens), F32),
            pltpu.VMEM((window, heads * tokens), BF16),
            pltpu.VMEM((window, heads * tokens), BF16),
            pltpu.VMEM((heads * tokens, dim), BF16),
            pltpu.VMEM((heads * tokens, dim), BF16),
        ],
        compiler_params=pltpu.CompilerParams(vmem_limit_bytes=56 * 2**20),
    )(first, ends, queries, grad_out, own, four, two, odd)


def local(doc_lengths, queries, key_rows, value_rows, grad_out):
    rows_dev = queries.shape[0]
    dev_rank = lax.axis_index(AXES)
    first_row = (dev_rank * rows_dev).astype(jnp.int32).reshape(1)
    doc_ends = jnp.cumsum(doc_lengths).astype(jnp.int32)
    spare = 128 - doc_lengths.shape[0]
    bounds = jnp.stack(
        [
            jnp.pad(doc_ends, (0, spare)),
            jnp.pad(doc_ends - doc_lengths, (0, spare), constant_values=-(2**30)),
        ]
    )
    bounds = jnp.pad(bounds, ((0, 6), (0, 0)))
    upper_core = dev_rank % 2 == 1
    upper_chip = dev_rank // 2 % 2 == 1

    own = jnp.stack([key_rows, value_rows])
    four = cyclic(own, 4)
    eight = cyclic(own, 8)
    two = swapped(
        jnp.where(upper_chip, jnp.stack([four, eight]), jnp.stack([own, four])), 2
    )
    odd = swapped(
        jnp.where(
            upper_core,
            jnp.stack([two[0], four, two[1], eight]),
            jnp.stack([own, two[0], four, two[1]]),
        ),
        1,
    )
    attn_out, grad_queries, even, far = attend(
        first_row, bounds, queries, grad_out, own, four, two, odd
    )
    back = swapped(far, 1).astype(F32)
    none = jnp.zeros_like(even[:1])
    even = jnp.concatenate([even, none]) + jnp.where(
        upper_core, jnp.concatenate([none, back]), jnp.concatenate([back, none])
    )
    back = swapped(jnp.stack([even[1], even[3]]).astype(BF16), 2).astype(F32)
    sum_zero = even[0] + jnp.where(upper_chip, 0.0, back[0])
    sum_four = even[2] + jnp.where(upper_chip, back[0], back[1])
    sum_eight = even[4] + jnp.where(upper_chip, back[1], 0.0)
    sums = (
        sum_zero
        + cyclic(sum_four.astype(BF16), -4).astype(F32)
        + cyclic(sum_eight.astype(BF16), -8).astype(F32)
    ).astype(BF16)
    return (attn_out, grad_queries, sums[0], sums[1])


def solution(mesh):
    split = P(AXES, None)
    return jax.shard_map(
        local,
        mesh=mesh,
        in_specs=(P(), split, split, split, split),
        out_specs=(split,) * 4,
        check_vma=False,
    )
```

```python
import functools
import math

import jax
import jax.numpy as jnp
from jax import lax
from jax.experimental import pallas as pl
from jax.experimental.pallas import tpu as pltpu
from jax.sharding import PartitionSpec as P

REACH = 8
AXES = ("dp", "ctx")
F32 = jnp.float32
BF16 = jnp.bfloat16
BIG = 1e30
SHAPE = jax.ShapeDtypeStruct


def cyclic(value, steps):
    count = lax.axis_size(AXES)
    return lax.ppermute(value, AXES, [(s, (s + steps) % count) for s in range(count)])


def swapped(value, bit):
    count = lax.axis_size(AXES)
    return lax.ppermute(value, AXES, [(s, s ^ bit) for s in range(count)])


def dot(a, b):
    return jnp.dot(a, b, preferred_element_type=F32)


def docs_kernel(place_ref, lengths_ref, docs_ref, mask_ref, gates_ref):
    tokens = docs_ref.shape[1]
    docs = lengths_ref.shape[0]
    gate = lax.broadcasted_iota(jnp.int32, gates_ref.shape, 0)
    gates_ref[...] = jnp.where(gate == 0, place_ref[1], place_ref[2]).astype(F32)
    lane = lax.broadcasted_iota(jnp.int32, gates_ref.shape, 1)
    starts = jnp.zeros(lane.shape, jnp.int32)
    ends = jnp.zeros(lane.shape, jnp.int32)
    for doc in range(docs):
        starts = starts + jnp.where(lane > doc, lengths_ref[doc], 0)
        ends = ends + jnp.where(lane >= doc, lengths_ref[doc], 0)
    starts = jnp.where(lane < docs, starts, -(2**30))[:1]
    ends = jnp.where(lane < docs, ends, 0)[:1]
    for back in range(REACH - 1, -1, -1):
        rows = lax.broadcasted_iota(jnp.int32, docs_ref.shape[1:], 0)
        at = place_ref[0] - back * tokens + rows
        inside = (at >= starts) & (at < ends)
        docs_ref[back] = jnp.where(inside, 1.0, 0.0).astype(BF16)
    mask_ref[...] = jnp.where(inside, 0.0, -BIG).T.astype(BF16)


def prep_kernel(mask_ref, q_ref, g_ref, k_ref, v_ref, qa_ref, gt_ref, k_own_ref, v_own_ref):
    tokens, dim = k_ref.shape
    k_own_ref[...] = k_ref[...]
    v_own_ref[...] = v_ref[...]
    for h in range(q_ref.shape[1] // dim):
        cols, span = slice(h * dim, (h + 1) * dim), slice(h * tokens, (h + 1) * tokens)
        qa_ref[:dim, span] = q_ref[:, cols].T
        qa_ref[dim:, span] = mask_ref[...]
        gt_ref[:, span] = g_ref[:, cols].T


def weigh_kernel(backs, groups, docs_ref, qa_ref, *refs):
    w_ref, top_ref, sum_ref, s_ref = refs[-4:]
    block_refs = refs[:groups]
    heads, tokens = top_ref.shape
    dim = qa_ref.shape[0] // 2
    blocks = [r.at[i] for r in block_refs for i in range(r.shape[0])]
    causal = lax.broadcasted_iota(jnp.int32, (tokens, tokens), 0) <= lax.broadcasted_iota(
        jnp.int32, (tokens, tokens), 1
    )
    unit = dim**-0.5 * math.log2(math.e)
    for h in range(heads):
        span = slice(h * tokens, (h + 1) * tokens)
        top = jnp.full((8, tokens), -jnp.inf, F32)
        for b, (back, block) in enumerate(zip(backs, blocks)):
            rows = slice(b * tokens, (b + 1) * tokens)
            s = dot(jnp.concatenate([block[...], docs_ref[back]], axis=1), qa_ref[:, span])
            if back == 0:
                s = jnp.where(causal, s, -BIG)
            s_ref[h % 2, rows, :] = s
            top = jnp.maximum(top, jnp.max(s.reshape(tokens // 8, 8, tokens), axis=0))
        row_max = jnp.max(top, axis=0, keepdims=True) * unit
        top_ref[h : h + 1, :] = row_max
        total = jnp.zeros((8, tokens), F32)
        for b in range(len(backs)):
            rows = slice(b * tokens, (b + 1) * tokens)
            w = jnp.exp2(s_ref[h % 2, rows, :] * unit - row_max)
            total = total + jnp.sum(w.reshape(tokens // 8, 8, tokens), axis=0)
            w_ref[rows, span] = w.astype(BF16)
        sum_ref[h : h + 1, :] = jnp.sum(total, axis=0, keepdims=True)


def value_kernel(
    wa_ref, wb_ref, wc_ref, ta_ref, tb_ref, tc_ref, la_ref, lb_ref, lc_ref, q_ref, g_ref, order_ref,
    coef_ref, qa_ref, qb_ref, qc_ref, even_ref, far_ref, g_div, flat,
):
    heads, tokens = ta_ref.shape
    dim = q_ref.shape[1] // heads
    row_max = jnp.maximum(jnp.maximum(ta_ref[...], tb_ref[...]), tc_ref[...])
    parts = [jnp.exp2(t[...] - row_max) for t in (ta_ref, tb_ref, tc_ref)]
    row_sum = sum(p * l[...] for p, l in zip(parts, (la_ref, lb_ref, lc_ref)))
    inverse = 1.0 / row_sum
    flat[...] = jnp.zeros_like(flat)
    for i, part in enumerate(parts):
        coef_ref[i] = part * inverse
        flat[i * heads : (i + 1) * heads, :] = part * inverse
    columns = flat[...].T
    for h in range(heads):
        cols, span = slice(h * dim, (h + 1) * dim), slice(h * tokens, (h + 1) * tokens)
        q = q_ref[:, cols].astype(F32) * dim**-0.5
        g = g_ref[:, cols].astype(F32)
        for i, qd_ref in enumerate((qa_ref, qb_ref, qc_ref)):
            column = columns[:, i * heads + h : i * heads + h + 1]
            qd_ref[span, :] = (q * column).astype(BF16)
            g_div[i, span, :] = (g * column).astype(BF16)
    for slot in range(REACH // 2):
        rows = slice(slot * tokens, (slot + 1) * tokens)
        far_ref[slot] = dot(wc_ref[rows, :], g_div[2]).astype(BF16)
    for slot in range(2):
        rows = slice(slot * tokens, (slot + 1) * tokens)
        even_ref[2 * slot + 1] = dot(wb_ref[rows, :], g_div[1])
        even_ref[2 * slot] = dot(wa_ref[rows, :], g_div[0])


def out_kernel(wa_ref, wb_ref, wc_ref, coef_ref, gt_ref, own_ref, four_ref, two_ref, odd_ref,
               o_ref, dot_ref, v_t):
    heads, tokens = coef_ref.shape[1:]
    dim = own_ref.shape[2]
    refs = (own_ref, four_ref, two_ref, odd_ref)
    for b, block in enumerate([r.at[i] for r in refs for i in range(r.shape[0])]):
        v_t[:, b * tokens : (b + 1) * tokens] = block[...].T
    for h in range(heads):
        cols, span = slice(h * dim, (h + 1) * dim), slice(h * tokens, (h + 1) * tokens)
        start, out = 0, 0.0
        for i, w_ref in enumerate((wa_ref, wb_ref, wc_ref)):
            stop = start + w_ref.shape[0]
            out = out + dot(v_t[:, start:stop], w_ref[:, span]) * coef_ref[i, h : h + 1, :]
            start = stop
        out = out.astype(BF16)
        o_ref[:, cols] = out.T
        dot_ref[h : h + 1, :] = jnp.sum(
            gt_ref[:, span].astype(F32) * out.astype(F32), axis=0, keepdims=True
        )


def score_terms(w_ref, gt_ref, dot_ref, qd_ref, blocks, ds_ref, outs):
    heads, tokens = dot_ref.shape
    for h in range(heads):
        span = slice(h * tokens, (h + 1) * tokens)
        for b, block in enumerate(blocks):
            rows = slice(b * tokens, (b + 1) * tokens)
            lean = dot(block[...], gt_ref[:, span]) - dot_ref[h : h + 1, :]
            ds_ref[rows, span] = (w_ref[rows, span].astype(F32) * lean).astype(BF16)
    for b, out in enumerate(outs):
        rows = slice(b * tokens, (b + 1) * tokens)
        out[...] = dot(ds_ref[rows, :], qd_ref[...]).astype(out.dtype)


def joined(upper, even, back):
    half = REACH // 2
    terms = [back[j].astype(F32) for j in range(half)]
    first = even[0] + jnp.where(upper, 0.0, terms[0])
    last = jnp.where(upper, terms[half - 1], 0.0)
    return [first] + [
        even[j] + jnp.where(upper, terms[j - 1], terms[j]) for j in range(1, half)
    ] + [last]


def far_kernel(gates_ref, w_ref, gt_ref, dot_ref, qd_ref, odd_ref, even_ref, back_ref,
               ds_ref, far_ref, send_ref, rest_ref):
    half = REACH // 2
    score_terms(
        w_ref, gt_ref, dot_ref, qd_ref, [odd_ref.at[i] for i in range(half)], ds_ref,
        [far_ref.at[i] for i in range(half)],
    )
    sums = joined(gates_ref[0:1, :] > 0, even_ref, back_ref)
    for i in range(2):
        send_ref[i] = sums[2 * i + 1].astype(BF16)
    for i in range(3):
        rest_ref[i] = sums[2 * i]


def mid_kernel(w_ref, gt_ref, dot_ref, qd_ref, two_ref, ds_ref, mid_ref):
    score_terms(
        w_ref, gt_ref, dot_ref, qd_ref, [two_ref.at[i] for i in range(2)], ds_ref,
        [mid_ref.at[i] for i in range(2)],
    )


def near_kernel(w_ref, gt_ref, dot_ref, qd_ref, own_ref, four_ref, order_ref, ds_ref, near_ref):
    score_terms(
        w_ref, gt_ref, dot_ref, qd_ref, [own_ref.at[0], four_ref.at[0]], ds_ref,
        [near_ref.at[i] for i in range(2)],
    )


def pair_kernel(gates_ref, own_ref, four_ref, eight_ref, order_ref, send_ref):
    upper = gates_ref[1:2, :] > 0
    send_ref[0] = jnp.where(upper, four_ref[...].astype(F32), own_ref[...].astype(F32)).astype(BF16)
    send_ref[1] = jnp.where(upper, eight_ref[...].astype(F32), four_ref[...].astype(F32)).astype(BF16)


def quad_kernel(gates_ref, own_ref, four_ref, eight_ref, two_ref, order_ref, send_ref):
    upper = gates_ref[0:1, :] > 0
    blocks = [own_ref, two_ref.at[0], four_ref, two_ref.at[1], eight_ref]
    wide = [block[...].astype(F32) for block in blocks]
    for i in range(REACH // 2):
        send_ref[i] = jnp.where(upper, wide[i + 1], wide[i]).astype(BF16)


def join_kernel(gates_ref, mid_ref, back_ref, send_ref):
    upper = gates_ref[0:1, :] > 0
    for i in range(2):
        back = jnp.where(upper, back_ref[2 * i].astype(F32), back_ref[2 * i + 1].astype(F32))
        send_ref[i] = (mid_ref[i] + back).astype(BF16)


def close_kernel(gates_ref, rest_ref, back_ref, order_ref, zero_ref, four_ref, eight_ref):
    upper = gates_ref[1:2, :] > 0
    back = [back_ref[i].astype(F32) for i in range(2)]
    zero_ref[...] = rest_ref[0] + jnp.where(upper, 0.0, back[0])
    four_ref[...] = (rest_ref[1] + jnp.where(upper, back[0], back[1])).astype(BF16)
    eight_ref[...] = (rest_ref[2] + jnp.where(upper, back[1], 0.0)).astype(BF16)


def near_close_kernel(gates_ref, near_ref, core_ref, chip_ref, order_ref, zero_ref, four_ref, eight_ref):
    other = gates_ref[0:1, :] > 0
    core = [core_ref[i].astype(F32) for i in range(REACH // 2)]
    upper = gates_ref[1:2, :] > 0
    back = [chip_ref[i].astype(F32) for i in range(2)]
    zero_ref[...] = near_ref[0] + jnp.where(other, 0.0, core[0]) + jnp.where(upper, 0.0, back[0])
    four = near_ref[1] + jnp.where(other, core[1], core[2])
    four_ref[...] = (four + jnp.where(upper, back[0], back[1])).astype(BF16)
    eight = jnp.where(other, core[3], 0.0)
    eight_ref[...] = (eight + jnp.where(upper, back[1], 0.0)).astype(BF16)


def query_kernel(
    da_ref, db_ref, dc_ref, coef_ref, own_ref, four_ref, two_ref, odd_ref, order_ref, dq_ref, k_t
):
    heads, tokens = coef_ref.shape[1:]
    dim = own_ref.shape[2]
    refs = (own_ref, four_ref, two_ref, odd_ref)
    for b, block in enumerate([r.at[i] for r in refs for i in range(r.shape[0])]):
        k_t[:, b * tokens : (b + 1) * tokens] = block[...].T
    for h in range(heads):
        cols, span = slice(h * dim, (h + 1) * dim), slice(h * tokens, (h + 1) * tokens)
        start, out = 0, 0.0
        for i, ds_ref in enumerate((da_ref, db_ref, dc_ref)):
            stop = start + ds_ref.shape[0]
            out = out + dot(k_t[:, start:stop], ds_ref[:, span]) * coef_ref[i, h : h + 1, :]
            start = stop
        dq_ref[:, cols] = (out * dim**-0.5).T.astype(BF16)


def call(kernel, outs, ins, scratch=(), us=1.0):
    vmem = pl.BlockSpec(memory_space=pltpu.VMEM)
    scalars = pl.BlockSpec(memory_space=pltpu.SMEM)
    return pl.pallas_call(
        kernel,
        out_shape=outs,
        in_specs=[scalars if x.ndim == 1 else vmem for x in ins],
        out_specs=(vmem,) * len(outs),
        scratch_shapes=scratch,
        compiler_params=pltpu.CompilerParams(vmem_limit_bytes=16 * 2**20),
        cost_estimate=pl.CostEstimate(
            flops=int(us * 1.0e7), bytes_accessed=1 << 20, transcendentals=0
        ),
    )(*ins)


def local(doc_lengths, queries, key_rows, value_rows, grad_out):
    tokens, width = queries.shape
    dim = key_rows.shape[1]
    heads = width // dim
    rows = heads * tokens
    half = REACH // 2
    rank = lax.axis_index(AXES)
    core, chip = rank % 2, rank // 2 % 2
    place = jnp.stack([rank * tokens, core, chip]).astype(jnp.int32)

    def block(count, kind=BF16):
        return SHAPE((count, tokens, dim), kind)

    one = SHAPE((tokens, dim), BF16)
    k_four, k_eight = cyclic(key_rows, 4), cyclic(key_rows, 8)
    docs, mask, gates = call(
        docs_kernel,
        (SHAPE((REACH, tokens, 128), BF16), SHAPE((128, tokens), BF16), SHAPE((8, 128), F32)),
        (place, doc_lengths),
        us=100,
    )
    q_aug, g_t, k_own, v_own = call(
        prep_kernel,
        (SHAPE((2 * dim, rows), BF16), SHAPE((dim, rows), BF16), one, one),
        (mask, queries, grad_out, key_rows, value_rows),
        us=1,
    )

    def weigh(backs, blocks, *order):
        span = len(backs) * tokens
        return call(
            functools.partial(weigh_kernel, backs, len(blocks)),
            (SHAPE((span, rows), BF16),) + (SHAPE((heads, tokens), F32),) * 2,
            (docs, q_aug) + blocks + order,
            [pltpu.VMEM((2, span, tokens), F32)],
            us=len(backs),
        )

    v_four, v_eight = cyclic(v_own, 4), cyclic(v_own, 8)
    (k_pair,) = call(pair_kernel, (block(2),), (gates, k_own, k_four, k_eight, k_own), us=0.1)
    k_two = swapped(k_pair, 2)
    wa, ta, la = weigh((0, 4), (k_own[None], k_four[None]), k_pair, v_four, v_eight)
    (k_quad,) = call(
        quad_kernel, (block(half),), (gates, k_own, k_four, k_eight, k_two, la), us=0.1
    )
    k_odd = swapped(k_quad, 1)
    wb, tb, lb = weigh((2, 6), (k_two,), k_quad)
    (v_pair,) = call(pair_kernel, (block(2),), (gates, v_own, v_four, v_eight, k_odd), us=0.1)
    v_two = swapped(v_pair, 2)
    wc, tc, lc = weigh((1, 3, 5, 7), (k_odd,), v_pair)
    (v_quad,) = call(
        quad_kernel, (block(half),), (gates, v_own, v_four, v_eight, v_two, lc), us=0.1
    )
    v_odd = swapped(v_quad, 1)
    coef, qd_a, qd_b, qd_c, v_even, v_far = call(
        value_kernel,
        (SHAPE((3, heads, tokens), F32),) + (SHAPE((rows, dim), BF16),) * 3
        + (block(half, F32), block(half)),
        (wa, wb, wc, ta, tb, tc, la, lb, lc, queries, grad_out, v_quad),
        [pltpu.VMEM((3, rows, dim), BF16), pltpu.VMEM((128, tokens), F32)],
        us=3,
    )
    v_back = swapped(v_far, 1)
    values = (value_rows[None], v_four[None], v_two, v_odd)
    attn_out, row_dot = call(
        out_kernel,
        (SHAPE((tokens, width), BF16), SHAPE((heads, tokens), F32)),
        (wa, wb, wc, coef, g_t) + values,
        [pltpu.VMEM((dim, REACH * tokens), BF16)],
        us=3,
    )
    ds_c, k_far, v_send, v_rest = call(
        far_kernel,
        (SHAPE((half * tokens, rows), BF16), block(half), block(2), block(3, F32)),
        (gates, wc, g_t, row_dot, qd_c, v_odd, v_even, v_back),
        us=3.5,
    )
    k_back = swapped(k_far, 1)
    v_back = swapped(v_send, 2)
    ds_b, k_mid = call(
        mid_kernel,
        (SHAPE((2 * tokens, rows), BF16), block(2, F32)),
        (wb, g_t, row_dot, qd_b, v_two),
        us=1.7,
    )
    (k_send,) = call(join_kernel, (block(2),), (gates, k_mid, k_back), us=0.1)
    k_chip = swapped(k_send, 2)
    ds_a, k_near = call(
        near_kernel,
        (SHAPE((2 * tokens, rows), BF16), block(2, F32)),
        (wa, g_t, row_dot, qd_a, value_rows[None], v_four[None], k_send),
        us=1.7,
    )
    closing = (SHAPE((tokens, dim), F32), one, one)
    v_zero, v_send_four, v_send_eight = call(
        close_kernel, closing, (gates, v_rest, v_back, k_near), us=0.1
    )
    v_from_four, v_from_eight = cyclic(v_send_four, -4), cyclic(v_send_eight, -8)
    k_zero, k_send_four, k_send_eight = call(
        near_close_kernel, closing, (gates, k_near, k_back, k_chip, v_send_eight), us=0.1
    )
    k_from_four, k_from_eight = cyclic(k_send_four, -4), cyclic(k_send_eight, -8)
    (grad_queries,) = call(
        query_kernel,
        (SHAPE((tokens, width), BF16),),
        (ds_a, ds_b, ds_c, coef, key_rows[None], k_four[None], k_two, k_odd, k_send_eight),
        [pltpu.VMEM((dim, REACH * tokens), BF16)],
        us=3,
    )
    grad_values = (v_zero + v_from_four.astype(F32) + v_from_eight.astype(F32)).astype(BF16)
    grad_keys = (k_zero + k_from_four.astype(F32) + k_from_eight.astype(F32)).astype(BF16)
    return (attn_out, grad_queries, grad_keys, grad_values)


def solution(mesh):
    split = P(AXES, None)
    return jax.shard_map(
        local,
        mesh=mesh,
        in_specs=(P(), split, split, split, split),
        out_specs=(split,) * 4,
        check_vma=False,
    )
```

```python
import functools
import math

import jax
import jax.numpy as jnp
from jax import lax
from jax.experimental import pallas as pl
from jax.experimental.pallas import tpu as pltpu
from jax.sharding import PartitionSpec as P

REACH = 8
AXES = ("dp", "ctx")
F32 = jnp.float32
BF16 = jnp.bfloat16
BIG = 1e30
SHAPE = jax.ShapeDtypeStruct


def cyclic(value, steps):
    count = lax.axis_size(AXES)
    pairs = [(s, (s + steps) % count) for s in range(count)]
    if abs(steps) == 8:
        pairs = [p for p in pairs if p[0] % 4]
    return lax.ppermute(value, AXES, pairs)


def swapped(value, bit):
    count = lax.axis_size(AXES)
    return lax.ppermute(value, AXES, [(s, s ^ bit) for s in range(count)])


def dot(a, b):
    return jnp.dot(a, b, preferred_element_type=F32)


def docs_kernel(place_ref, lengths_ref, docs_ref, mask_ref, gates_ref):
    tokens = docs_ref.shape[1]
    docs = lengths_ref.shape[0]
    gate = lax.broadcasted_iota(jnp.int32, gates_ref.shape, 0)
    gates_ref[...] = jnp.where(gate == 0, place_ref[1], place_ref[2]).astype(F32)
    lane = lax.broadcasted_iota(jnp.int32, gates_ref.shape, 1)
    starts = jnp.zeros(lane.shape, jnp.int32)
    ends = jnp.zeros(lane.shape, jnp.int32)
    for doc in range(docs):
        starts = starts + jnp.where(lane > doc, lengths_ref[doc], 0)
        ends = ends + jnp.where(lane >= doc, lengths_ref[doc], 0)
    starts = jnp.where(lane < docs, starts, -(2**30))[:1]
    ends = jnp.where(lane < docs, ends, 0)[:1]
    for back in range(REACH - 1, -1, -1):
        rows = lax.broadcasted_iota(jnp.int32, docs_ref.shape[1:], 0)
        at = place_ref[0] - back * tokens + rows
        inside = (at >= starts) & (at < ends)
        docs_ref[back] = jnp.where(inside, 1.0, 0.0).astype(BF16)
    mask_ref[...] = jnp.where(inside, 0.0, -BIG).T.astype(BF16)


def prep_kernel(mask_ref, q_ref, g_ref, k_ref, v_ref, qa_ref, gt_ref, k_own_ref, v_own_ref):
    tokens, dim = k_ref.shape
    k_own_ref[...] = k_ref[...]
    v_own_ref[...] = v_ref[...]
    for h in range(q_ref.shape[1] // dim):
        cols, span = slice(h * dim, (h + 1) * dim), slice(h * tokens, (h + 1) * tokens)
        qa_ref[:dim, span] = q_ref[:, cols].T
        qa_ref[dim:, span] = mask_ref[...]
        gt_ref[:, span] = g_ref[:, cols].T


def weigh_kernel(backs, groups, docs_ref, qa_ref, *refs):
    w_ref, top_ref, sum_ref, s_ref = refs[-4:]
    block_refs = refs[:groups]
    heads, tokens = top_ref.shape
    dim = qa_ref.shape[0] // 2
    blocks = [r.at[i] for r in block_refs for i in range(r.shape[0])]
    causal = lax.broadcasted_iota(jnp.int32, (tokens, tokens), 0) <= lax.broadcasted_iota(
        jnp.int32, (tokens, tokens), 1
    )
    unit = dim**-0.5 * math.log2(math.e)
    for h in range(heads):
        span = slice(h * tokens, (h + 1) * tokens)
        top = jnp.full((8, tokens), -jnp.inf, F32)
        for b, (back, block) in enumerate(zip(backs, blocks)):
            rows = slice(b * tokens, (b + 1) * tokens)
            s = dot(jnp.concatenate([block[...], docs_ref[back]], axis=1), qa_ref[:, span])
            if back == 0:
                s = jnp.where(causal, s, -BIG)
            s_ref[h % 2, rows, :] = s
            top = jnp.maximum(top, jnp.max(s.reshape(tokens // 8, 8, tokens), axis=0))
        row_max = jnp.max(top, axis=0, keepdims=True) * unit
        top_ref[h : h + 1, :] = row_max
        total = jnp.zeros((8, tokens), F32)
        for b in range(len(backs)):
            rows = slice(b * tokens, (b + 1) * tokens)
            w = jnp.exp2(s_ref[h % 2, rows, :] * unit - row_max)
            total = total + jnp.sum(w.reshape(tokens // 8, 8, tokens), axis=0)
            w_ref[rows, span] = w.astype(BF16)
        sum_ref[h : h + 1, :] = jnp.sum(total, axis=0, keepdims=True)


def value_kernel(
    wa_ref, wb_ref, wc_ref, ta_ref, tb_ref, tc_ref, la_ref, lb_ref, lc_ref, q_ref, g_ref, order_ref,
    coef_ref, qa_ref, qb_ref, qc_ref, even_ref, far_ref, g_div, flat,
):
    heads, tokens = ta_ref.shape
    dim = q_ref.shape[1] // heads
    row_max = jnp.maximum(jnp.maximum(ta_ref[...], tb_ref[...]), tc_ref[...])
    parts = [jnp.exp2(t[...] - row_max) for t in (ta_ref, tb_ref, tc_ref)]
    row_sum = sum(p * l[...] for p, l in zip(parts, (la_ref, lb_ref, lc_ref)))
    inverse = 1.0 / row_sum
    flat[...] = jnp.zeros_like(flat)
    for i, part in enumerate(parts):
        coef_ref[i] = part * inverse
        flat[i * heads : (i + 1) * heads, :] = part * inverse
    columns = flat[...].T
    for h in range(heads):
        cols, span = slice(h * dim, (h + 1) * dim), slice(h * tokens, (h + 1) * tokens)
        q = q_ref[:, cols].astype(F32) * dim**-0.5
        g = g_ref[:, cols].astype(F32)
        for i, qd_ref in enumerate((qa_ref, qb_ref, qc_ref)):
            column = columns[:, i * heads + h : i * heads + h + 1]
            qd_ref[span, :] = (q * column).astype(BF16)
            g_div[i, span, :] = (g * column).astype(BF16)
    for slot in range(REACH // 2):
        rows = slice(slot * tokens, (slot + 1) * tokens)
        far_ref[slot] = dot(wc_ref[rows, :], g_div[2]).astype(BF16)
    for slot in range(2):
        rows = slice(slot * tokens, (slot + 1) * tokens)
        even_ref[2 * slot + 1] = dot(wb_ref[rows, :], g_div[1])
        even_ref[2 * slot] = dot(wa_ref[rows, :], g_div[0])


def out_kernel(wa_ref, wb_ref, wc_ref, coef_ref, gt_ref, own_ref, four_ref, two_ref, odd_ref,
               o_ref, dot_ref, v_t):
    heads, tokens = coef_ref.shape[1:]
    dim = own_ref.shape[2]
    refs = (own_ref, four_ref, two_ref, odd_ref)
    for b, block in enumerate([r.at[i] for r in refs for i in range(r.shape[0])]):
        v_t[:, b * tokens : (b + 1) * tokens] = block[...].T
    for h in range(heads):
        cols, span = slice(h * dim, (h + 1) * dim), slice(h * tokens, (h + 1) * tokens)
        start, out = 0, 0.0
        for i, w_ref in enumerate((wa_ref, wb_ref, wc_ref)):
            stop = start + w_ref.shape[0]
            out = out + dot(v_t[:, start:stop], w_ref[:, span]) * coef_ref[i, h : h + 1, :]
            start = stop
        out = out.astype(BF16)
        o_ref[:, cols] = out.T
        dot_ref[h : h + 1, :] = jnp.sum(
            gt_ref[:, span].astype(F32) * out.astype(F32), axis=0, keepdims=True
        )


def score_terms(w_ref, gt_ref, dot_ref, qd_ref, blocks, ds_ref, outs):
    heads, tokens = dot_ref.shape
    for h in range(heads):
        span = slice(h * tokens, (h + 1) * tokens)
        for b, block in enumerate(blocks):
            rows = slice(b * tokens, (b + 1) * tokens)
            lean = dot(block[...], gt_ref[:, span]) - dot_ref[h : h + 1, :]
            ds_ref[rows, span] = (w_ref[rows, span].astype(F32) * lean).astype(BF16)
    for b, out in enumerate(outs):
        rows = slice(b * tokens, (b + 1) * tokens)
        out[...] = dot(ds_ref[rows, :], qd_ref[...]).astype(out.dtype)


def joined(upper, even, back):
    half = REACH // 2
    terms = [back[j].astype(F32) for j in range(half)]
    first = even[0] + jnp.where(upper, 0.0, terms[0])
    last = jnp.where(upper, terms[half - 1], 0.0)
    return [first] + [
        even[j] + jnp.where(upper, terms[j - 1], terms[j]) for j in range(1, half)
    ] + [last]


def far_kernel(gates_ref, w_ref, gt_ref, dot_ref, qd_ref, odd_ref, even_ref, back_ref,
               ds_ref, far_ref, send_ref, rest_ref):
    half = REACH // 2
    score_terms(
        w_ref, gt_ref, dot_ref, qd_ref, [odd_ref.at[i] for i in range(half)], ds_ref,
        [far_ref.at[i] for i in range(half)],
    )
    sums = joined(gates_ref[0:1, :] > 0, even_ref, back_ref)
    for i in range(2):
        send_ref[i] = sums[2 * i + 1].astype(BF16)
    for i in range(3):
        rest_ref[i] = sums[2 * i]


def mid_kernel(w_ref, gt_ref, dot_ref, qd_ref, two_ref, ds_ref, mid_ref):
    score_terms(
        w_ref, gt_ref, dot_ref, qd_ref, [two_ref.at[i] for i in range(2)], ds_ref,
        [mid_ref.at[i] for i in range(2)],
    )


def near_kernel(w_ref, gt_ref, dot_ref, qd_ref, own_ref, four_ref, order_ref, ds_ref, near_ref):
    score_terms(
        w_ref, gt_ref, dot_ref, qd_ref, [own_ref.at[0], four_ref.at[0]], ds_ref,
        [near_ref.at[i] for i in range(2)],
    )


def pair_kernel(gates_ref, own_ref, four_ref, eight_ref, *refs):
    send_ref = refs[-1]
    upper = gates_ref[1:2, :] > 0
    send_ref[0] = jnp.where(upper, four_ref[...].astype(F32), own_ref[...].astype(F32)).astype(BF16)
    send_ref[1] = jnp.where(upper, eight_ref[...].astype(F32), four_ref[...].astype(F32)).astype(BF16)


def quad_kernel(gates_ref, own_ref, four_ref, eight_ref, two_ref, order_ref, send_ref):
    upper = gates_ref[0:1, :] > 0
    blocks = [own_ref, two_ref.at[0], four_ref, two_ref.at[1], eight_ref]
    wide = [block[...].astype(F32) for block in blocks]
    for i in range(REACH // 2):
        send_ref[i] = jnp.where(upper, wide[i + 1], wide[i]).astype(BF16)


def join_kernel(gates_ref, mid_ref, back_ref, send_ref):
    upper = gates_ref[0:1, :] > 0
    for i in range(2):
        back = jnp.where(upper, back_ref[2 * i].astype(F32), back_ref[2 * i + 1].astype(F32))
        send_ref[i] = (mid_ref[i] + back).astype(BF16)


def close_kernel(gates_ref, rest_ref, back_ref, order_ref, zero_ref, four_ref, eight_ref):
    upper = gates_ref[1:2, :] > 0
    back = [back_ref[i].astype(F32) for i in range(2)]
    zero_ref[...] = rest_ref[0] + jnp.where(upper, 0.0, back[0])
    four_ref[...] = (rest_ref[1] + jnp.where(upper, back[0], back[1])).astype(BF16)
    eight_ref[...] = (rest_ref[2] + jnp.where(upper, back[1], 0.0)).astype(BF16)


def near_close_kernel(gates_ref, near_ref, core_ref, chip_ref, order_ref, zero_ref, four_ref, eight_ref):
    other = gates_ref[0:1, :] > 0
    core = [core_ref[i].astype(F32) for i in range(REACH // 2)]
    upper = gates_ref[1:2, :] > 0
    back = [chip_ref[i].astype(F32) for i in range(2)]
    zero_ref[...] = near_ref[0] + jnp.where(other, 0.0, core[0]) + jnp.where(upper, 0.0, back[0])
    four = near_ref[1] + jnp.where(other, core[1], core[2])
    four_ref[...] = (four + jnp.where(upper, back[0], back[1])).astype(BF16)
    eight = jnp.where(other, core[3], 0.0)
    eight_ref[...] = (eight + jnp.where(upper, back[1], 0.0)).astype(BF16)


def query_kernel(
    da_ref, db_ref, dc_ref, coef_ref, own_ref, four_ref, two_ref, odd_ref, order_ref, dq_ref, k_t
):
    heads, tokens = coef_ref.shape[1:]
    dim = own_ref.shape[2]
    refs = (own_ref, four_ref, two_ref, odd_ref)
    for b, block in enumerate([r.at[i] for r in refs for i in range(r.shape[0])]):
        k_t[:, b * tokens : (b + 1) * tokens] = block[...].T
    for h in range(heads):
        cols, span = slice(h * dim, (h + 1) * dim), slice(h * tokens, (h + 1) * tokens)
        start, out = 0, 0.0
        for i, ds_ref in enumerate((da_ref, db_ref, dc_ref)):
            stop = start + ds_ref.shape[0]
            out = out + dot(k_t[:, start:stop], ds_ref[:, span]) * coef_ref[i, h : h + 1, :]
            start = stop
        dq_ref[:, cols] = (out * dim**-0.5).T.astype(BF16)


def call(kernel, outs, ins, scratch=(), us=1.0):
    vmem = pl.BlockSpec(memory_space=pltpu.VMEM)
    scalars = pl.BlockSpec(memory_space=pltpu.SMEM)
    return pl.pallas_call(
        kernel,
        out_shape=outs,
        in_specs=[scalars if x.ndim == 1 else vmem for x in ins],
        out_specs=(vmem,) * len(outs),
        scratch_shapes=scratch,
        compiler_params=pltpu.CompilerParams(vmem_limit_bytes=16 * 2**20),
        cost_estimate=pl.CostEstimate(
            flops=int(us * 1.0e7), bytes_accessed=1 << 20, transcendentals=0
        ),
    )(*ins)


def local(doc_lengths, queries, key_rows, value_rows, grad_out):
    tokens, width = queries.shape
    dim = key_rows.shape[1]
    heads = width // dim
    rows = heads * tokens
    half = REACH // 2
    rank = lax.axis_index(AXES)
    core, chip = rank % 2, rank // 2 % 2
    place = jnp.stack([rank * tokens, core, chip]).astype(jnp.int32)

    def block(count, kind=BF16):
        return SHAPE((count, tokens, dim), kind)

    one = SHAPE((tokens, dim), BF16)
    both = jnp.stack([key_rows, value_rows])
    four, eight = cyclic(both, 4), cyclic(both, 8)
    (k_four, v_four), (k_eight, v_eight) = four, eight
    docs, mask, gates = call(
        docs_kernel,
        (SHAPE((REACH, tokens, 128), BF16), SHAPE((128, tokens), BF16), SHAPE((8, 128), F32)),
        (place, doc_lengths),
        us=100,
    )
    q_aug, g_t, k_own, v_own = call(
        prep_kernel,
        (SHAPE((2 * dim, rows), BF16), SHAPE((dim, rows), BF16), one, one),
        (mask, queries, grad_out, key_rows, value_rows),
        us=1,
    )

    def weigh(backs, blocks, *order):
        span = len(backs) * tokens
        return call(
            functools.partial(weigh_kernel, backs, len(blocks)),
            (SHAPE((span, rows), BF16),) + (SHAPE((heads, tokens), F32),) * 2,
            (docs, q_aug) + blocks + order,
            [pltpu.VMEM((2, span, tokens), F32)],
            us=len(backs),
        )

    (k_pair,) = call(pair_kernel, (block(2),), (gates, k_own, k_four, k_eight), us=0.1)
    k_two = swapped(k_pair, 2)
    wa, ta, la = weigh((0, 4), (k_own[None], k_four[None]), k_pair)
    (k_quad,) = call(
        quad_kernel, (block(half),), (gates, k_own, k_four, k_eight, k_two, la), us=0.1
    )
    k_odd = swapped(k_quad, 1)
    wb, tb, lb = weigh((2, 6), (k_two,), k_quad)
    (v_pair,) = call(pair_kernel, (block(2),), (gates, v_own, v_four, v_eight, k_quad), us=0.1)
    v_two = swapped(v_pair, 2)
    wc, tc, lc = weigh((1, 3, 5, 7), (k_odd,), v_pair)
    (v_quad,) = call(
        quad_kernel, (block(half),), (gates, v_own, v_four, v_eight, v_two, lc), us=0.1
    )
    v_odd = swapped(v_quad, 1)
    coef, qd_a, qd_b, qd_c, v_even, v_far = call(
        value_kernel,
        (SHAPE((3, heads, tokens), F32),) + (SHAPE((rows, dim), BF16),) * 3
        + (block(half, F32), block(half)),
        (wa, wb, wc, ta, tb, tc, la, lb, lc, queries, grad_out, v_quad),
        [pltpu.VMEM((3, rows, dim), BF16), pltpu.VMEM((128, tokens), F32)],
        us=3,
    )
    v_back = swapped(v_far, 1)
    values = (value_rows[None], v_four[None], v_two, v_odd)
    attn_out, row_dot = call(
        out_kernel,
        (SHAPE((tokens, width), BF16), SHAPE((heads, tokens), F32)),
        (wa, wb, wc, coef, g_t) + values,
        [pltpu.VMEM((dim, REACH * tokens), BF16)],
        us=3,
    )
    ds_c, k_far, v_send, v_rest = call(
        far_kernel,
        (SHAPE((half * tokens, rows), BF16), block(half), block(2), block(3, F32)),
        (gates, wc, g_t, row_dot, qd_c, v_odd, v_even, v_back),
        us=3.5,
    )
    k_back = swapped(k_far, 1)
    v_back = swapped(v_send, 2)
    ds_b, k_mid = call(
        mid_kernel,
        (SHAPE((2 * tokens, rows), BF16), block(2, F32)),
        (wb, g_t, row_dot, qd_b, v_two),
        us=1.7,
    )
    (k_send,) = call(join_kernel, (block(2),), (gates, k_mid, k_back), us=0.1)
    k_chip = swapped(k_send, 2)
    ds_a, k_near = call(
        near_kernel,
        (SHAPE((2 * tokens, rows), BF16), block(2, F32)),
        (wa, g_t, row_dot, qd_a, value_rows[None], v_four[None], k_send),
        us=1.7,
    )
    closing = (SHAPE((tokens, dim), F32), one, one)
    v_zero, v_send_four, v_send_eight = call(
        close_kernel, closing, (gates, v_rest, v_back, k_near), us=0.1
    )
    v_from_four, v_from_eight = cyclic(v_send_four, -4), cyclic(v_send_eight, -8)
    k_zero, k_send_four, k_send_eight = call(
        near_close_kernel, closing, (gates, k_near, k_back, k_chip, v_send_eight), us=0.1
    )
    k_from_four, k_from_eight = cyclic(k_send_four, -4), cyclic(k_send_eight, -8)
    (grad_queries,) = call(
        query_kernel,
        (SHAPE((tokens, width), BF16),),
        (ds_a, ds_b, ds_c, coef, key_rows[None], k_four[None], k_two, k_odd, k_send_eight),
        [pltpu.VMEM((dim, REACH * tokens), BF16)],
        us=3,
    )
    grad_values = (v_zero + v_from_four.astype(F32) + v_from_eight.astype(F32)).astype(BF16)
    grad_keys = (k_zero + k_from_four.astype(F32) + k_from_eight.astype(F32)).astype(BF16)
    return (attn_out, grad_queries, grad_keys, grad_values)


def solution(mesh):
    split = P(AXES, None)
    return jax.shard_map(
        local,
        mesh=mesh,
        in_specs=(P(), split, split, split, split),
        out_specs=(split,) * 4,
        check_vma=False,
    )
```
